512 devices in a mesh: blk: 128 (over y_hi, x, z), grp: 4 (over y_lo, core).
Axes of the slice: x: 4, y: 4 (y_hi: 2, y_lo: 2; y = y_hi * 2 + y_lo), z: 16, core: 2. Of those that a mesh axis runs over, the one named last changes fastest.
Arguments:
- orbitals: bfloat16 [3072, 2, 8, 128], P(('blk', 'grp')), may hold values from -2.390625 to 2.390625
- screen: bfloat16 [128, 24, 2, 128, 128], P('blk', 'grp'), may hold values from -0.375 to 0.375
- slot_of_q: int32 [3, 24], replicated, may hold values from 0 to 23, as said below
Outputs:
- lower: bfloat16 [128, 3, 2, 384, 384], P('blk', None, None, None, 'grp')
- upper: bfloat16 [128, 2, 2, 384, 384], P('blk', None, None, 'grp')
The draws below stay inside these ranges and needn't reach their ends.
Inputs may be any that keep to these rules, and one draw needn't show every extreme that they name: Each row of slot_of_q is a permutation of 0 to 23.
All inputs are finite; a program needn't handle non-finite values.
Results may differ from the reference program's by a relative error of at most 0.0064.
Values may be sent and summed in bfloat16 or wider, within the bound.
A program may use at most 64 MiB of HBM per device.

```python
import jax
import jax.numpy as jnp
from jax import lax

P_SIZE = 16
NBAND = 8
NMU = 128
KB = 24
STEPS = 3
NK = 3072


def draw_slot_of_q(key, part):
    key = jax.random.fold_in(key, 11)
    scores = jax.random.randint(key, (STEPS, KB), 0, 1 << 20) * KB + jnp.arange(KB, dtype=jnp.int32)
    return jnp.argsort(scores, axis=-1).astype(jnp.int32)


def block_scale(rng, extent, cuts, least, top_value):
    level, own = 1.0, jax.random.fold_in(rng, 6)
    for position, shards_of in cuts:
        draws = jnp.exp(jax.random.uniform(jax.random.fold_in(own, position), (shards_of,), jnp.float32, least / len(cuts), top_value / len(cuts)))
        level = level * jnp.repeat(draws, extent[position] // shards_of).reshape([-1 if axis == position else 1 for axis in range(len(extent))])
    return level


def scatter_about(rng, dims, spread, most, split=(), kind=jnp.bfloat16):
    array = spread * jax.random.normal(rng, dims, jnp.float32)
    if split:
        array = array * block_scale(rng, dims, split, -0.22, 0.18)
    return jnp.clip(array, -most, most).astype(kind)


def setup_inputs(seed: int = 0) -> dict:
    arg_keys = jax.random.split(jax.random.key(seed), 4)
    orbitals = scatter_about(arg_keys[0], (NK, 2, NBAND, NMU), 0.4, 2.390625, ((0, 512),))
    screen = scatter_about(arg_keys[1], (NK // KB, KB, 2, NMU, NMU), (2 * NMU) ** -0.5, 0.375, ((0, 128), (1, 4)))
    slot_of_q = draw_slot_of_q(jax.random.fold_in(arg_keys[3], 71), 0)
    return {"orbitals": orbitals, "screen": screen, "slot_of_q": slot_of_q}


def pair_kernel(rolled_rows, partner_row, screen_by_q):
    half_bands = rolled_rows.shape[2] // 2
    count_q = rolled_rows.shape[0]
    points = rolled_rows.shape[3]

    def densities(first_band, last_band):
        first_real = rolled_rows[:, 0, first_band:last_band, None, :]
        first_imag = rolled_rows[:, 1, first_band:last_band, None, :]
        second_real = partner_row[0, first_band:last_band][None, None]
        second_imag = partner_row[1, first_band:last_band][None, None]
        real_part = first_real * second_real + first_imag * second_imag
        imag_part = first_real * second_imag - first_imag * second_real
        real_part = real_part.reshape(count_q, half_bands * half_bands, points).astype(jnp.bfloat16)
        imag_part = imag_part.reshape(count_q, half_bands * half_bands, points).astype(jnp.bfloat16)
        return real_part.astype(jnp.float32), imag_part.astype(jnp.float32)

    cond_real, cond_imag = densities(half_bands, 2 * half_bands)
    val_real, val_imag = densities(0, half_bands)
    screen_real = screen_by_q[:, 0]
    screen_imag = screen_by_q[:, 1]
    mixed_real = (jnp.einsum('qam,qmn->qan', cond_real, screen_real) - jnp.einsum('qam,qmn->qan', cond_imag, screen_imag)).astype(jnp.bfloat16).astype(jnp.float32)
    mixed_imag = (jnp.einsum('qam,qmn->qan', cond_real, screen_imag) + jnp.einsum('qam,qmn->qan', cond_imag, screen_real)).astype(jnp.bfloat16).astype(jnp.float32)
    kernel_real = jnp.einsum('qan,qbn->qab', mixed_real, val_real) + jnp.einsum('qan,qbn->qab', mixed_imag, val_imag)
    kernel_imag = jnp.einsum('qan,qbn->qab', mixed_imag, val_real) - jnp.einsum('qan,qbn->qab', mixed_real, val_imag)
    stacked = jnp.stack([kernel_real, kernel_imag]).reshape(2, count_q, half_bands, half_bands, half_bands, half_bands)
    stacked = stacked.transpose(0, 1, 2, 4, 3, 5)
    return stacked.reshape(2, count_q, half_bands * half_bands, half_bands * half_bands).astype(jnp.bfloat16)


def reference(orbitals, screen, slot_of_q):
    block_count = NK // KB
    orbital_rows = orbitals.reshape(block_count, KB, 2, NBAND, NMU)
    block_ids = jnp.arange(block_count, dtype=jnp.int32)
    ramp = jnp.arange(KB, dtype=jnp.int32)
    lower_list = []
    for cycle_step in range(STEPS):
        screen_by_q = jnp.take(screen[cycle_step], slot_of_q[cycle_step], axis=0).astype(jnp.float32)

        def build(block_id):
            left_rows = orbital_rows[block_id].astype(jnp.float32)
            partner = jnp.mod(block_id - cycle_step, block_count).astype(jnp.int32)
            right_rows = orbital_rows[partner].astype(jnp.float32)

            def column(second_point):
                forward = jnp.mod(second_point + ramp, KB).astype(jnp.int32)
                kernel_q = pair_kernel(jnp.take(left_rows, forward, axis=0), right_rows[second_point], screen_by_q)
                backward = jnp.mod(ramp - second_point, KB).astype(jnp.int32)
                return jnp.take(kernel_q, backward, axis=1)

            columns = lax.map(column, ramp)
            return columns.transpose(1, 2, 3, 0, 4).reshape(2, KB * P_SIZE, KB * P_SIZE)

        lower_list.append(lax.map(build, block_ids))
    lower = jnp.stack(lower_list, axis=1)
    upper_list = []
    for offset in range(1, STEPS):
        rolled = jnp.roll(lower[:, offset], -offset, axis=0)
        upper_list.append(jnp.stack([jnp.swapaxes(rolled[:, 0], 1, 2), -jnp.swapaxes(rolled[:, 1], 1, 2)], axis=1))
    upper = jnp.stack(upper_list, axis=1)
    return (lower, upper)
```

```python
import functools
import jax
import jax.numpy as jnp
from jax import lax
from jax.experimental import pallas as pl
from jax.experimental.pallas import tpu as pltpu
from jax.sharding import PartitionSpec as P

BF = jnp.bfloat16
F32 = jnp.float32


def select_matrix(tile):
    r = lax.broadcasted_iota(jnp.int32, (256, 128), 0)
    col = lax.broadcasted_iota(jnp.int32, (256, 128), 1)
    band = (r % 4) if tile else ((r // 4) % 4)
    return (col == (r // 16) * 8 + 4 + band).astype(F32).astype(BF)


def expand_rows(x, dst, stage, sel):
    x2 = x.reshape(384, 128)
    for i in range(3):
        dst[pl.ds(i * 256, 256), :] = jnp.dot(sel, x2[i * 128:(i + 1) * 128], preferred_element_type=F32)
    stage[...] = x2.astype(F32)


def valence(stage, dst):
    for p in range(2):
        for v in range(4):
            dst[p * 4 + v] = stage[pl.ds(p * 8 + v, 24, stride=16), :]


def expand_cols(x, dst, pt, sel):
    x2 = x.reshape(96, 128)
    dst[...] = jnp.dot(sel[:192, :96], x2, preferred_element_type=F32)
    n = lax.broadcasted_iota(jnp.int32, (8, 128), 0)
    l = lax.broadcasted_iota(jnp.int32, (8, 128), 1)
    g = (n == l % 4).astype(F32)
    dn = (((0,), (0,)), ((), ()))
    for j in range(6):
        a = lax.dot_general(x[j, 0].astype(F32), g, dn, preferred_element_type=F32).astype(BF)
        b = lax.dot_general(x[j, 1].astype(F32), g, dn, preferred_element_type=F32).astype(BF)
        pt[j, 0:128, 0:128] = a
        pt[j, 0:128, 128:256] = -b
        pt[j, 128:256, 0:128] = b
        pt[j, 128:256, 128:256] = a


def mix(load_w, slot_ref, s, g6, jobs):
    def step(q, carry):
        wr, wi = load_w(slot_ref[s, q])
        wc = jnp.concatenate([jnp.concatenate([wr, wi], 1), jnp.concatenate([-wi, wr], 1)], 0)
        rows = []
        for urep, utile, _, _ in jobs:
            for j in range(6):
                k = lax.rem(g6 + j + q, 24)
                at = pl.multiple_of(k * 32, 32)
                ar = urep[pl.ds(at, 16), :]
                ai = urep[pl.ds(at + 16, 16), :]
                br = utile[j * 32:j * 32 + 16, :]
                bi = utile[j * 32 + 16:j * 32 + 32, :]
                rows.append(jnp.concatenate([(ar * br + ai * bi).astype(BF), (ar * bi - ai * br).astype(BF)], 1))
        y = jnp.dot(jnp.concatenate(rows, 0), wc, preferred_element_type=F32)
        for n, (_, _, yr, yi) in enumerate(jobs):
            for j in range(6):
                k = lax.rem(g6 + j + q, 24)
                r0 = (n * 6 + j) * 16
                yr[pl.ds(j * 384 + k, 16, stride=24), :] = y[r0:r0 + 16, 0:128]
                yi[pl.ds(j * 384 + k, 16, stride=24), :] = y[r0:r0 + 16, 128:256]
        return carry
    lax.fori_loop(0, 24, step, 0, unroll=8)


def close(yr, yi, uv, pt, acc, tr, ti):
    lane = lax.broadcasted_iota(jnp.int32, (256, 256), 1) % 128 // 4

    def step(j, carry):
        ur = uv[0:4]
        ui = uv[4:8]
        p = pt[j]
        weights = jnp.concatenate([jnp.where(lane == j * 4 + c2, p, jnp.zeros_like(p)) for c2 in range(4)], 0)
        blocks = []
        for c in range(4):
            parts = []
            for c2 in range(4):
                at = pl.multiple_of(j * 384 + (c * 4 + c2) * 24, 8)
                a = yr[pl.ds(at, 24), :][None]
                b = yi[pl.ds(at, 24), :][None]
                parts.append((a * ur - b * ui).reshape(96, 128).astype(BF))
                parts.append((a * ui + b * ur).reshape(96, 128).astype(BF))
            blocks.append(jnp.concatenate(parts, 1))
        d = jnp.dot(jnp.concatenate(blocks, 0), weights, preferred_element_type=F32)

        acc[...] += d
        return carry
    acc[...] = jnp.zeros_like(acc)
    lax.fori_loop(0, 6, step, 0, unroll=6)
    for cv in range(16):
        tr[pl.ds(cv, 24, stride=16), :] = acc[cv * 24:cv * 24 + 24, 0:128]
        ti[pl.ds(cv, 24, stride=16), :] = acc[cv * 24:cv * 24 + 24, 128:256]


def emit_lower(tr, ti, out, s):
    out[0, s, 0] = tr[:, 0:96].astype(BF)
    out[0, s, 1] = ti[:, 0:96].astype(BF)


def emit_upper(tr, ti, out, t):
    out[0, t, 0] = tr[...].T[0:96, :].astype(BF)
    out[0, t, 1] = (-ti[...]).T[0:96, :].astype(BF)


def scratch():
    return dict(
        urep=[pltpu.VMEM((768, 128), F32)] * 3,
        uv=[pltpu.VMEM((8, 24, 128), F32)] * 3,
        utile=[pltpu.VMEM((192, 128), F32)] * 3,
        pt=[pltpu.VMEM((6, 256, 256), BF)] * 3,
        stage=pltpu.VMEM((384, 128), F32),
        yr=[pltpu.VMEM((2304, 128), F32)] * 2,
        yi=[pltpu.VMEM((2304, 128), F32)] * 2,
        acc=pltpu.VMEM((384, 256), F32),
        tr=pltpu.VMEM((384, 128), F32),
        ti=pltpu.VMEM((384, 128), F32),
    )


MESH = pl.DeviceIdType.MESH


def place():
    b = lax.axis_index("blk")
    g = lax.axis_index("grp")
    return (b // 16) % 4, (b // 64) * 2 + g // 2, b % 16, g % 2


def at_chip(x, y, z, c):
    x, y, z = lax.rem(x, 4), lax.rem(y, 4), lax.rem(z, 16)
    return (y // 2) * 64 + x * 16 + z, (y % 2) * 2 + c


class Exchange:
    def __init__(self, screen, orb, wbuf, rows, subs, sems):
        self.screen, self.orb, self.wbuf, self.rows, self.subs = screen, orb, wbuf, rows, subs
        self.sems = sems
        self.x, self.y, self.z, self.c = place()
        self.b, self.g = lax.axis_index("blk"), lax.axis_index("grp")
        self.h = jnp.where((self.y == 1) | (self.y == 2), 1, 0)
        self.yh = self.y // 2
        self.source = (self.x == 0) & (self.y < 2) & (self.z < 3)
        self.pending = []

    def row(self, off):
        return lax.rem(self.b + off + 128, 128)

    def barrier(self):
        bar = pltpu.get_barrier_semaphore()
        x, y, z, c = self.x, self.y, self.z, self.c
        near = [at_chip(x + d, y, z, c) for d in (1, 2, 3)] + [at_chip(x, y + d, z, c) for d in (1, 2, 3)]
        near += [at_chip(x, y, z + d, c) for d in (1, 2, 3, 13, 14, 15)]
        near += [(self.b, lax.rem(self.g + d, 4)) for d in (1, 2, 3)]
        near += [(self.row(d), self.g) for d in (1, 2, -1, -2)]
        for d in near:
            pl.semaphore_signal(bar, inc=1, device_id=d, device_id_type=MESH)

        @pl.when(self.source)
        def _():
            for xx in range(4):
                for yh in range(2):
                    if xx or yh:
                        pl.semaphore_signal(bar, inc=1, device_id=self.target(xx, yh), device_id_type=MESH)

        @pl.when((z < 3) & jnp.logical_not(self.source))
        def _():
            pl.semaphore_signal(bar, inc=1, device_id=at_chip(0, self.h, z, c), device_id_type=MESH)
        extra = jnp.where(self.source, 7, jnp.where(z < 3, 1, 0))
        pl.semaphore_wait(bar, len(near) + extra)

    def target(self, xx, yh):
        return at_chip(xx, self.y if yh == 0 else 3 - self.y, self.z, self.c)

    def remote(self, src, dst, send, recv, to):
        return pltpu.make_async_remote_copy(src_ref=src, dst_ref=dst, send_sem=send, recv_sem=recv, device_id=to, device_id_type=MESH)

    def launch(self, cp, cond=None):
        if cond is None:
            cp.start()
        else:
            pl.when(cond)(lambda: cp.start())
        self.pending.append((cp, cond))

    def unit(self, half, x):
        return pl.ds(half * 12 + x * 3, 3)

    def own(self, s, half):
        return self.wbuf.at[s, self.h, self.c, self.yh, self.unit(half, self.x)]

    def scatter(self):
        sm, z = self.sems, self.z

        @pl.when(self.source)
        def _():
            for half in range(2):
                for xx, yh in ((2, 1), (1, 1), (3, 1), (2, 0), (1, 0), (3, 0), (0, 1)):
                    self.remote(self.screen.at[yh, self.unit(half, xx)], self.wbuf.at[z, self.h, self.c, yh, self.unit(half, xx)],
                                sm["scat"].at[half, xx, yh], sm["own"].at[z, half], self.target(xx, yh)).start()
                pltpu.make_async_copy(self.screen.at[0, self.unit(half, 0)], self.wbuf.at[z, self.h, self.c, 0, self.unit(half, 0)],
                                      sm["own"].at[z, half]).start()

    def drain_scatter(self):
        @pl.when(self.source)
        def _():
            for half in range(2):
                for xx, yh in ((2, 1), (1, 1), (3, 1), (2, 0), (1, 0), (3, 0), (0, 1)):
                    self.remote(self.screen.at[yh, self.unit(half, xx)], self.wbuf.at[self.z, self.h, self.c, yh, self.unit(half, xx)],
                                self.sems["scat"].at[half, xx, yh], self.sems["own"].at[self.z, half], self.target(xx, yh)).wait_send()

    def orbitals_out(self):
        sm, g = self.sems, self.g
        self.o_in = []
        local = [pltpu.make_async_copy(self.orb, self.rows.at[0, pl.ds(g * 6, 6)], sm["oloc"].at[0]),
                 pltpu.make_async_copy(self.orb, self.subs.at[0], sm["oloc"].at[1])]
        for cp in local:
            cp.start()
        self.o_local = local
        for n, (off, dst) in enumerate(((-1, self.rows.at[1, pl.ds(g * 6, 6)]), (-2, self.rows.at[2, pl.ds(g * 6, 6)]),
                                        (1, self.subs.at[1]), (2, self.subs.at[2]))):
            cp = self.remote(self.orb, dst, sm["os"].at[n], sm["or"].at[n], (self.row(off), g))
            self.launch(cp)
            self.o_in.append(cp)
        self.group_out(0, self.orb, 4)

    def group_out(self, r, src, base):
        for d in (1, 2, 3):
            n = base + d - 1
            cp = self.remote(src, self.rows.at[r, pl.ds(self.g * 6, 6)], self.sems["os"].at[n], self.sems["or"].at[n],
                             (self.b, lax.rem(self.g + d, 4)))
            self.launch(cp)
            back = lax.rem(self.g + 4 - d, 4)
            self.o_in.append(self.remote(src, self.rows.at[r, pl.ds(back * 6, 6)], self.sems["os"].at[n], self.sems["or"].at[n],
                                         (self.b, lax.rem(self.g + d, 4))))

    def orbitals_on(self):
        for r in (1, 2):
            self.o_in[r - 1].wait_recv()
            self.group_out(r, self.rows.at[r, pl.ds(self.g * 6, 6)], 4 + 3 * r)

    def orbitals_done(self):
        for cp in self.o_local:
            cp.wait()
        for cp in self.o_in[2:]:
            cp.wait_recv()

    def first(self, s):
        sm, x, y, z, c = self.sems, self.x, self.y, self.z, self.c
        dz = lax.rem(z + 16 - s, 16)
        hub = (dz == 0) | (dz == 3) | (dz == 6) | (dz == 10) | (dz == 13)
        hops = ((3, (dz == 0) | (dz == 3)), (13, (dz == 0) | (dz == 13)), (2, dz == 6), (1, hub), (15, hub))
        for half in range(2):
            mine = self.own(s, half)
            self.remote(mine, mine, sm["zs"].at[s, 0, half], sm["own"].at[s, half], (self.b, self.g)).wait_recv()
            for n, (off, cond) in enumerate(hops):
                self.launch(self.remote(mine, mine, sm["zs"].at[s, n, half], sm["own"].at[s, half], at_chip(x, y, z + off, c)), cond)
        for half in range(2):
            mine = self.own(s, half)
            for d in (2, 1, 3):
                to = at_chip(x + d, y, z, c) if half == 0 else at_chip(x, y + d, z, c)
                self.launch(self.remote(mine, mine, sm["p1s"].at[s, half, d - 1], sm["p1r"].at[s, half, d - 1], to))

    def split(self, y):
        return jnp.where((y == 1) | (y == 2), 1, 0), y // 2

    def second(self, s):
        sm, x, y, z, c = self.sems, self.x, self.y, self.z, self.c
        for half in range(2):
            for d in (1, 3, 2):
                if half == 0:
                    there = self.wbuf.at[s, self.h, c, self.yh, self.unit(0, lax.rem(x + 4 - d, 4))]
                else:
                    hh, yy = self.split(lax.rem(y + 4 - d, 4))
                    there = self.wbuf.at[s, hh, c, yy, self.unit(1, x)]
                self.remote(there, there, sm["p1s"].at[s, half, d - 1], sm["p1r"].at[s, half, d - 1], (self.b, self.g)).wait_recv()
            if half == 0:
                mine = self.wbuf.at[s, self.h, c, self.yh, pl.ds(0, 12)]
            else:
                mine = self.wbuf.at[s, :, c, :, self.unit(1, x)]
            for d in (2, 1, 3):
                to = at_chip(x, y + d, z, c) if half == 0 else at_chip(x + d, y, z, c)
                self.launch(self.remote(mine, mine, sm["p2s"].at[s, half, d - 1], sm["p2r"].at[s, half, d - 1], to))

    def third(self, s):
        sm, x, y, z, c = self.sems, self.x, self.y, self.z, self.c
        for half in range(2):
            for d in (1, 3, 2):
                if half == 0:
                    hh, yy = self.split(lax.rem(y + 4 - d, 4))
                    there = self.wbuf.at[s, hh, c, yy, pl.ds(0, 12)]
                else:
                    there = self.wbuf.at[s, :, c, :, self.unit(1, lax.rem(x + 4 - d, 4))]
                self.remote(there, there, sm["p2s"].at[s, half, d - 1], sm["p2r"].at[s, half, d - 1], (self.b, self.g)).wait_recv()
        mine = self.wbuf.at[s, :, c]
        self.launch(self.remote(mine, mine, sm["cs"].at[s], sm["cr"].at[s], at_chip(x, y, z, 1 - c)))

    def ready(self, s):
        there = self.wbuf.at[s, :, 1 - self.c]
        self.remote(there, there, self.sems["cs"].at[s], self.sems["cr"].at[s], (self.b, self.g)).wait_recv()

    def finish(self):
        self.drain_scatter()
        for cp, cond in self.pending:
            if cond is None:
                cp.wait_send()
            else:
                pl.when(cond)(lambda cp=cp: cp.wait_send())


def exchange_sems():
    D = pltpu.SemaphoreType.DMA
    return {"scat": D((2, 4, 2)), "own": D((3, 2)), "zs": D((3, 5, 2)), "p1s": D((3, 2, 3)), "p1r": D((3, 2, 3)),
            "p2s": D((3, 2, 3)), "p2r": D((3, 2, 3)), "cs": D((3,)), "cr": D((3,)), "os": D((13,)), "or": D((13,)), "oloc": D((2,))}


def exchange_kernel(tree, screen, orb, wbuf, rows, subs, *flat):
    ex = Exchange(screen, orb, wbuf, rows, subs, jax.tree.unflatten(tree, flat))
    ex.barrier()
    ex.scatter()
    ex.orbitals_out()
    ex.first(1)
    ex.first(2)
    ex.second(1)
    ex.first(0)
    ex.second(2)
    ex.orbitals_on()
    ex.third(1)
    ex.second(0)
    ex.third(2)
    ex.third(0)
    ex.orbitals_done()
    for s in range(3):
        ex.ready(s)
    ex.finish()


def compute_kernel(tree, slot_ref, rows_ref, subs_ref, w_ref, lower, upper, *flat):
    sc = jax.tree.unflatten(tree, flat)
    g6 = lax.axis_index("grp") * 6
    rep, tile = select_matrix(False), select_matrix(True)
    for r in range(3):
        expand_rows(rows_ref[r], sc["urep"][r], sc["stage"], rep)
        valence(sc["stage"], sc["uv"][r])
        expand_cols(subs_ref[r], sc["utile"][r], sc["pt"][r], tile)
    for s in (1, 2, 0):
        jobs = [(sc["urep"][0], sc["utile"][s], sc["yr"][0], sc["yi"][0])]
        if s:
            jobs.append((sc["urep"][s], sc["utile"][0], sc["yr"][1], sc["yi"][1]))

        def load_w(slot):
            part = slot // 3
            w = w_ref[s, part // 4, part // 2 % 2, part % 2, pl.ds(slot % 3 * 8, 8)]
            return w[0:4].reshape(128, 128), w[4:8].reshape(128, 128)
        mix(load_w, slot_ref, s, g6, jobs)
        close(sc["yr"][0], sc["yi"][0], sc["uv"][0], sc["pt"][s], sc["acc"], sc["tr"], sc["ti"])
        emit_lower(sc["tr"], sc["ti"], lower, s)
        if s:
            close(sc["yr"][1], sc["yi"][1], sc["uv"][s], sc["pt"][0], sc["acc"], sc["tr"], sc["ti"])
            emit_upper(sc["tr"], sc["ti"], upper, s - 1)


def body(orbitals, screen, slot_of_q):
    vmem = pl.BlockSpec(memory_space=pltpu.VMEM)
    leaves, tree = jax.tree.flatten(exchange_sems())
    w, rows, subs = pl.pallas_call(
        functools.partial(exchange_kernel, tree),
        out_shape=[
            jax.ShapeDtypeStruct((3, 2, 2, 2, 24, 32, 128), BF),
            jax.ShapeDtypeStruct((3, 24, 2, 8, 128), BF),
            jax.ShapeDtypeStruct((3, 6, 2, 8, 128), BF),
        ],
        in_specs=[vmem] * 2,
        out_specs=[vmem] * 3,
        scratch_shapes=leaves,
        compiler_params=pltpu.CompilerParams(collective_id=0, has_side_effects=True, vmem_limit_bytes=40 << 20),
        name="exchange",
    )(screen.reshape(2, 24, 32, 128), orbitals)
    leaves, tree = jax.tree.flatten(scratch())
    return pl.pallas_call(
        functools.partial(compute_kernel, tree),
        out_shape=[
            jax.ShapeDtypeStruct((1, 3, 2, 384, 96), BF),
            jax.ShapeDtypeStruct((1, 2, 2, 96, 384), BF),
        ],
        in_specs=[pl.BlockSpec(memory_space=pltpu.SMEM)] + [vmem] * 3,
        out_specs=[vmem] * 2,
        scratch_shapes=leaves,
        compiler_params=pltpu.CompilerParams(vmem_limit_bytes=48 << 20),
        name="pairs",
    )(slot_of_q, rows, subs, w)


def solution(mesh):
    in_specs = (P(("blk", "grp"), None, None, None), P("blk", "grp", None, None, None), P())
    out_specs = (P("blk", None, None, None, "grp"), P("blk", None, None, "grp", None))
    return jax.shard_map(body, mesh=mesh, in_specs=in_specs, out_specs=out_specs, check_vma=False)
```

```python
import functools
import jax
import jax.numpy as jnp
from jax import lax
from jax.experimental import pallas as pl
from jax.experimental.pallas import tpu as pltpu
from jax.sharding import PartitionSpec as P

BF = jnp.bfloat16
F32 = jnp.float32


def select_matrix(tile):
    r = lax.broadcasted_iota(jnp.int32, (256, 128), 0)
    col = lax.broadcasted_iota(jnp.int32, (256, 128), 1)
    band = (r % 4) if tile else ((r // 4) % 4)
    return (col == (r // 16) * 8 + 4 + band).astype(F32).astype(BF)


def expand_rows(x, dst, stage, sel):
    x2 = x.reshape(384, 128)
    for i in range(3):
        dst[pl.ds(i * 256, 256), :] = jnp.dot(sel, x2[i * 128:(i + 1) * 128], preferred_element_type=F32)
    stage[...] = x2.astype(F32)


def valence(stage, dst):
    for p in range(2):
        for v in range(4):
            dst[p * 4 + v] = stage[pl.ds(p * 8 + v, 24, stride=16), :]


def expand_cols(x, dst, pt, sel):
    x2 = x.reshape(96, 128)
    dst[...] = jnp.dot(sel[:192, :96], x2, preferred_element_type=F32)
    n = lax.broadcasted_iota(jnp.int32, (8, 128), 0)
    l = lax.broadcasted_iota(jnp.int32, (8, 128), 1)
    g = (n == l % 4).astype(F32)
    dn = (((0,), (0,)), ((), ()))
    for j in range(6):
        a = lax.dot_general(x[j, 0].astype(F32), g, dn, preferred_element_type=F32).astype(BF)
        b = lax.dot_general(x[j, 1].astype(F32), g, dn, preferred_element_type=F32).astype(BF)
        pt[j, 0:128, 0:128] = a
        pt[j, 0:128, 128:256] = -b
        pt[j, 128:256, 0:128] = b
        pt[j, 128:256, 128:256] = a


def mix(load_w, slot_ref, s, g6, jobs):
    def step(q, carry):
        wr, wi = load_w(slot_ref[s, q])
        wc = jnp.concatenate([jnp.concatenate([wr, wi], 1), jnp.concatenate([-wi, wr], 1)], 0)
        rows = []
        for urep, utile, _, _ in jobs:
            for j in range(6):
                k = lax.rem(g6 + j + q, 24)
                at = pl.multiple_of(k * 32, 32)
                ar = urep[pl.ds(at, 16), :]
                ai = urep[pl.ds(at + 16, 16), :]
                br = utile[j * 32:j * 32 + 16, :]
                bi = utile[j * 32 + 16:j * 32 + 32, :]
                rows.append(jnp.concatenate([(ar * br + ai * bi).astype(BF), (ar * bi - ai * br).astype(BF)], 1))
        y = jnp.dot(jnp.concatenate(rows, 0), wc, preferred_element_type=F32)
        for n, (_, _, yr, yi) in enumerate(jobs):
            for j in range(6):
                k = lax.rem(g6 + j + q, 24)
                r0 = (n * 6 + j) * 16
                yr[pl.ds(j * 384 + k, 16, stride=24), :] = y[r0:r0 + 16, 0:128]
                yi[pl.ds(j * 384 + k, 16, stride=24), :] = y[r0:r0 + 16, 128:256]
        return carry
    lax.fori_loop(0, 24, step, 0, unroll=8)


def close(yr, yi, uv, pt, acc, tr, ti):
    lane = lax.broadcasted_iota(jnp.int32, (256, 256), 1) % 128 // 4

    def step(j, carry):
        ur = uv[0:4]
        ui = uv[4:8]
        p = pt[j]
        weights = jnp.concatenate([jnp.where(lane == j * 4 + c2, p, jnp.zeros_like(p)) for c2 in range(4)], 0)
        blocks = []
        for c in range(4):
            parts = []
            for c2 in range(4):
                at = pl.multiple_of(j * 384 + (c * 4 + c2) * 24, 8)
                a = yr[pl.ds(at, 24), :][None]
                b = yi[pl.ds(at, 24), :][None]
                parts.append((a * ur - b * ui).reshape(96, 128).astype(BF))
                parts.append((a * ui + b * ur).reshape(96, 128).astype(BF))
            blocks.append(jnp.concatenate(parts, 1))
        d = jnp.dot(jnp.concatenate(blocks, 0), weights, preferred_element_type=F32)

        acc[...] += d
        return carry
    acc[...] = jnp.zeros_like(acc)
    lax.fori_loop(0, 6, step, 0, unroll=6)
    for cv in range(16):
        tr[pl.ds(cv, 24, stride=16), :] = acc[cv * 24:cv * 24 + 24, 0:128]
        ti[pl.ds(cv, 24, stride=16), :] = acc[cv * 24:cv * 24 + 24, 128:256]


def emit_lower(tr, ti, out, s):
    out[0, s, 0] = tr[...].T[0:96, :].astype(BF)
    out[0, s, 1] = ti[...].T[0:96, :].astype(BF)


def emit_upper(tr, ti, out, t):
    out[0, t, 0] = tr[...].T[0:96, :].astype(BF)
    out[0, t, 1] = (-ti[...]).T[0:96, :].astype(BF)


def scratch():
    return dict(
        urep=[pltpu.VMEM((768, 128), F32)] * 3,
        uv=[pltpu.VMEM((8, 24, 128), F32)] * 3,
        utile=[pltpu.VMEM((192, 128), F32)] * 3,
        pt=[pltpu.VMEM((6, 256, 256), BF)] * 3,
        stage=pltpu.VMEM((384, 128), F32),
        yr=[pltpu.VMEM((2304, 128), F32)] * 2,
        yi=[pltpu.VMEM((2304, 128), F32)] * 2,
        acc=pltpu.VMEM((384, 256), F32),
        tr=pltpu.VMEM((384, 128), F32),
        ti=pltpu.VMEM((384, 128), F32),
    )


MESH = pl.DeviceIdType.MESH


def place():
    b = lax.axis_index("blk")
    g = lax.axis_index("grp")
    return (b // 16) % 4, (b // 64) * 2 + g // 2, b % 16, g % 2


def at_chip(x, y, z, c):
    x, y, z = lax.rem(x, 4), lax.rem(y, 4), lax.rem(z, 16)
    return (y // 2) * 64 + x * 16 + z, (y % 2) * 2 + c


class Exchange:
    def __init__(self, screen, orb, wbuf, rows, subs, sems):
        self.screen, self.orb, self.wbuf, self.rows, self.subs = screen, orb, wbuf, rows, subs
        self.sems = sems
        self.x, self.y, self.z, self.c = place()
        self.b, self.g = lax.axis_index("blk"), lax.axis_index("grp")
        self.h = jnp.where((self.y == 1) | (self.y == 2), 1, 0)
        self.yh = self.y // 2
        self.source = (self.x == 0) & (self.y < 2) & (self.z < 3)
        self.pending = []

    def row(self, off):
        return lax.rem(self.b + off + 128, 128)

    def signal(self, sem, to, cond=None):
        def go():
            pl.semaphore_signal(sem, inc=1, device_id=to, device_id_type=MESH)
        if cond is None:
            go()
        else:
            pl.when(cond)(go)

    def barrier(self):
        bar = pltpu.get_barrier_semaphore()
        x, y, z, c, g = self.x, self.y, self.z, self.c, self.g
        near = [at_chip(x + d, y, z, c) for d in (1, 2, 3)] + [at_chip(x, y + d, z, c) for d in (1, 2, 3)]
        near += [(self.b, lax.rem(g + d, 4)) for d in (1, 2, 3)]
        for d in near:
            self.signal(bar, d)

        @pl.when(self.source)
        def _():
            for xx in range(4):
                for yh in range(2):
                    if xx or yh:
                        self.signal(bar, self.target(xx, yh))
        self.signal(bar, at_chip(0, self.h, z, c), (z < 3) & jnp.logical_not(self.source))
        for k in (1, 2, 3):
            self.signal(bar, at_chip(x, y, z + k, c), z + k < 16)
        self.signal(bar, at_chip(x, y, 15, c), z == 0)
        self.signal(bar, (self.row(-1), g), z == 0)
        self.signal(bar, (self.row(-2), g), z < 2)
        count = len(near) + jnp.where(self.source, 7, jnp.where(z < 3, 1, 0))
        count += jnp.minimum(z, 3) + jnp.where(z == 15, 3, jnp.where(z == 14, 1, 0))
        pl.semaphore_wait(bar, count)
        for k in (1, 2, 3):
            self.signal(self.sems["rdyz"].at[k - 1], at_chip(x, y, z + 16 - k, c), z >= k)
        self.signal(self.sems["rdyw"], at_chip(x, y, 0, c), z == 15)
        self.signal(self.sems["rdyr"].at[0], (self.row(1), g), z == 15)
        self.signal(self.sems["rdyr"].at[1], (self.row(2), g), z >= 14)

    def await_up(self, s, only=None):
        z = self.z
        for k in (1, 2, 3):
            early = {1: ((z == 1) & (k < 3)) | ((z == 3) & (k != 2)) | (z == 6) | ((z == 12) & (k == 1)),
                     2: (z == 2) & (k == 1), 0: z == 0}
            if s is None:
                cond = (z + k < 16) & jnp.logical_not(early[0] | early[1] | early[2])
            else:
                cond = early[s] if only is None else early[s] & only
            pl.when(cond)(lambda k=k: pl.semaphore_wait(self.sems["rdyz"].at[k - 1], 1))

    def target(self, xx, yh):
        return at_chip(xx, self.y if yh == 0 else 3 - self.y, self.z, self.c)

    def remote(self, src, dst, send, recv, to):
        return pltpu.make_async_remote_copy(src_ref=src, dst_ref=dst, send_sem=send, recv_sem=recv, device_id=to, device_id_type=MESH)

    def launch(self, cp, cond=None):
        if cond is None:
            cp.start()
        else:
            pl.when(cond)(lambda: cp.start())
        self.pending.append((cp, cond))

    def unit(self, half, x):
        return pl.ds(half * 12 + x * 3, 3)

    def own(self, s, half):
        return self.wbuf[s].at[self.h, self.c, self.yh, self.unit(half, self.x)]

    def scattered(self, s):
        sm = self.sems
        for half in range(2):
            for xx, yh in ((2, 1), (1, 1), (3, 1), (2, 0), (1, 0), (3, 0), (0, 1)):
                yield self.remote(self.screen.at[yh, self.unit(half, xx)], self.wbuf[s].at[self.h, self.c, yh, self.unit(half, xx)],
                                  sm["scat"].at[half, xx, yh], sm["own"].at[s, half], self.target(xx, yh))

    def scatter(self):
        for s in range(3):
            @pl.when(self.source & (self.z == s))
            def _():
                for cp in self.scattered(s):
                    cp.start()
                for half in range(2):
                    pltpu.make_async_copy(self.screen.at[0, self.unit(half, 0)], self.wbuf[s].at[self.h, self.c, 0, self.unit(half, 0)],
                                          self.sems["own"].at[s, half]).start()

    def drain_scatter(self):
        for s in range(3):
            @pl.when(self.source & (self.z == s))
            def _():
                for cp in self.scattered(s):
                    cp.wait_send()

    def orbitals_out(self):
        sm, g = self.sems, self.g
        self.o_in = []
        self.o_local = [pltpu.make_async_copy(self.orb, self.rows.at[0, pl.ds(g * 6, 6)], sm["oloc"].at[0]),
                        pltpu.make_async_copy(self.orb, self.subs.at[0], sm["oloc"].at[1])]
        for cp in self.o_local:
            cp.start()
        self.o_row = []
        for n, (off, dst) in enumerate(((-1, self.rows.at[1, pl.ds(g * 6, 6)]), (-2, self.rows.at[2, pl.ds(g * 6, 6)]),
                                        (1, self.subs.at[1]), (2, self.subs.at[2]))):
            self.o_row.append(self.remote(self.orb, dst, sm["os"].at[n], sm["or"].at[n], (self.row(off), g)))
        self.group_out(0, self.orb, 4)
        z = self.z
        self.launch(self.o_row[0], z >= 1)
        self.launch(self.o_row[1], z >= 2)
        self.launch(self.o_row[2], z == 15)
        self.launch(self.o_row[3], z >= 14)

    def orbitals_up(self):
        self.launch(self.o_row[2], self.z < 15)
        self.launch(self.o_row[3], self.z < 14)

    def orbitals_wrap(self):
        z = self.z
        pl.when(z == 0)(lambda: pl.semaphore_wait(self.sems["rdyr"].at[0], 1))
        pl.when(z < 2)(lambda: pl.semaphore_wait(self.sems["rdyr"].at[1], 1))
        self.launch(self.o_row[0], z == 0)
        self.launch(self.o_row[1], z < 2)

    def group_out(self, r, src, base):
        for d in (1, 2, 3):
            n = base + d - 1
            cp = self.remote(src, self.rows.at[r, pl.ds(self.g * 6, 6)], self.sems["os"].at[n], self.sems["or"].at[n],
                             (self.b, lax.rem(self.g + d, 4)))
            self.launch(cp)
            back = lax.rem(self.g + 4 - d, 4)
            self.o_in.append(self.remote(src, self.rows.at[r, pl.ds(back * 6, 6)], self.sems["os"].at[n], self.sems["or"].at[n],
                                         (self.b, lax.rem(self.g + d, 4))))

    def orbitals_on(self):
        for r in (1, 2):
            self.o_row[r - 1].wait_recv()
            self.group_out(r, self.rows.at[r, pl.ds(self.g * 6, 6)], 4 + 3 * r)

    def orbitals_done(self):
        for cp in self.o_local:
            cp.wait()
        for cp in self.o_row[2:] + self.o_in:
            cp.wait_recv()

    def first(self, s, only=None):
        sm, x, y, z, c = self.sems, self.x, self.y, self.z, self.c
        hops = ((3, (z == 3) | (z == 6) | (z == (0 if s == 0 else 3))), (2, (z == 6) | (z == (s if s < 2 else 6))),
                (15, (z == 6) | (z == 15) | (z == 12) | (z == (s if s else 6))), (13, z == 15),
                (1, (z == 3) | (z == 6) | (z == 12) | (z == s)), (14, (z == 12) | (z == (2 if s == 2 else 12))))
        for half in range(2):
            mine = self.own(s, half)
            cp = self.remote(mine, mine, sm["zs"].at[s, 0, half], sm["own"].at[s, half], (self.b, self.g))
            if only is None:
                cp.wait_recv()
            else:
                pl.when(only)(cp.wait_recv)
            if half == 0:
                self.await_up(s, only)
            for n, (off, cond) in enumerate(hops):
                cond = cond if only is None else cond & only
                self.launch(self.remote(mine, mine, sm["zs"].at[s, n, half], sm["own"].at[s, half], at_chip(x, y, z + off, c)), cond)
            for d in (2, 1, 3):
                to = at_chip(x + d, y, z, c) if half == 0 else at_chip(x, y + d, z, c)
                self.launch(self.remote(mine, mine, sm["p1s"].at[s, half, d - 1], sm["p1r"].at[s, half, d - 1], to), only)

    def down(self, s):
        sm, z = self.sems, self.z
        if s == 1:
            pl.when(z == 0)(lambda: pl.semaphore_wait(sm["rdyw"], 1))
        for half in range(2):
            mine = self.own(s, half)
            self.launch(self.remote(mine, mine, sm["ds"].at[s, half], sm["own"].at[s, half], at_chip(self.x, self.y, 15, self.c)), z == 0)

    def split(self, y):
        return jnp.where((y == 1) | (y == 2), 1, 0), y // 2

    def part(self, s, half, d, c):
        if half == 0:
            hh, yy = self.split(lax.rem(self.y + 4 - d, 4))
            return self.wbuf[s].at[hh, c, yy, pl.ds(0, 12)]
        return self.wbuf[s].at[:, c, :, self.unit(1, lax.rem(self.x + 4 - d, 4))]

    def to_sibling(self, s, half, d):
        mine = self.part(s, half, d, self.c)
        self.launch(self.remote(mine, mine, self.sems["cs"].at[s, half, d], self.sems["cr"].at[s, half, d],
                                at_chip(self.x, self.y, self.z, 1 - self.c)))

    def second(self, s):
        sm, x, y, z, c = self.sems, self.x, self.y, self.z, self.c
        for half in range(2):
            for d in (1, 3, 2):
                if half == 0:
                    there = self.wbuf[s].at[self.h, c, self.yh, self.unit(0, lax.rem(x + 4 - d, 4))]
                else:
                    hh, yy = self.split(lax.rem(y + 4 - d, 4))
                    there = self.wbuf[s].at[hh, c, yy, self.unit(1, x)]
                self.remote(there, there, sm["p1s"].at[s, half, d - 1], sm["p1r"].at[s, half, d - 1], (self.b, self.g)).wait_recv()
            mine = self.part(s, half, 0, c)
            for d in (2, 1, 3):
                to = at_chip(x, y + d, z, c) if half == 0 else at_chip(x + d, y, z, c)
                self.launch(self.remote(mine, mine, sm["p2s"].at[s, half, d - 1], sm["p2r"].at[s, half, d - 1], to))
            self.to_sibling(s, half, 0)

    def third(self, s, steps):
        sm = self.sems
        for d in steps:
            for half in range(2):
                there = self.part(s, half, d, self.c)
                self.remote(there, there, sm["p2s"].at[s, half, d - 1], sm["p2r"].at[s, half, d - 1], (self.b, self.g)).wait_recv()
                self.to_sibling(s, half, d)

    def ready(self, s):
        for d in (0, 1, 3, 2):
            for half in range(2):
                there = self.part(s, half, d, 1 - self.c)
                self.remote(there, there, self.sems["cs"].at[s, half, d], self.sems["cr"].at[s, half, d], (self.b, self.g)).wait_recv()

    def finish(self):
        self.drain_scatter()
        for cp, cond in self.pending:
            if cond is None:
                cp.wait_send()
            else:
                pl.when(cond)(lambda cp=cp: cp.wait_send())


def exchange_sems():
    D = pltpu.SemaphoreType.DMA
    return {"scat": D((2, 4, 2)), "own": D((3, 2)), "zs": D((3, 6, 2)), "p1s": D((3, 2, 3)), "p1r": D((3, 2, 3)),
            "p2s": D((3, 2, 3)), "p2r": D((3, 2, 3)), "cs": D((3, 2, 4)), "cr": D((3, 2, 4)), "ds": D((3, 2)), "os": D((13,)), "or": D((13,)), "oloc": D((2,)),
            "rdyz": pltpu.SemaphoreType.REGULAR((3,)), "rdyw": pltpu.SemaphoreType.REGULAR, "rdyr": pltpu.SemaphoreType.REGULAR((2,))}


def buffers():
    return {"w": [pltpu.VMEM((2, 2, 2, 24, 32, 128), BF)] * 3, "rows": pltpu.VMEM((3, 24, 2, 8, 128), BF), "subs": pltpu.VMEM((3, 6, 2, 8, 128), BF),
            "slot": pltpu.SMEM((3, 24), jnp.int32), "slot_sem": pltpu.SemaphoreType.DMA}


def kernel(tree, slot_ref, screen, orb, lower, upper, *flat):
    sc, buf, sems = jax.tree.unflatten(tree, flat)
    w_ref, slot_sm = buf["w"], buf["slot"]
    g6 = lax.axis_index("grp") * 6
    ex = Exchange(screen, orb, w_ref, buf["rows"], buf["subs"], sems)

    def prepare():
        rep, tile = select_matrix(False), select_matrix(True)
        for r in range(3):
            expand_rows(buf["rows"][r], sc["urep"][r], sc["stage"], rep)
            valence(sc["stage"], sc["uv"][r])
            expand_cols(buf["subs"][r], sc["utile"][r], sc["pt"][r], tile)

    def jobs_of(s):
        jobs = [(sc["urep"][0], sc["utile"][s], sc["yr"][0], sc["yi"][0])]
        if s:
            jobs.append((sc["urep"][s], sc["utile"][0], sc["yr"][1], sc["yi"][1]))
        return jobs

    def mixed(s):
        def load_w(slot):
            part = slot // 3
            w = w_ref[s][part // 4, part // 2 % 2, part % 2, pl.ds(slot % 3 * 8, 8)]
            return w[0:4].reshape(128, 128), w[4:8].reshape(128, 128)
        mix(load_w, slot_sm, s, g6, jobs_of(s))

    def low(s):
        close(sc["yr"][0], sc["yi"][0], sc["uv"][0], sc["pt"][s], sc["acc"], sc["tr"], sc["ti"])
        emit_lower(sc["tr"], sc["ti"], lower, s)

    def high(s):
        close(sc["yr"][1], sc["yi"][1], sc["uv"][s], sc["pt"][0], sc["acc"], sc["tr"], sc["ti"])
        emit_upper(sc["tr"], sc["ti"], upper, s - 1)

    slots = pltpu.make_async_copy(slot_ref, slot_sm, buf["slot_sem"])
    slots.start()
    ex.barrier()
    ex.scatter()
    ex.orbitals_out()
    ex.first(1)
    ex.first(2)
    ex.first(0, ex.z == 0)
    ex.down(1)
    ex.down(2)
    ex.down(0)
    ex.second(1)
    ex.first(0, ex.z > 0)
    ex.await_up(None)
    ex.orbitals_up()
    ex.second(2)
    ex.orbitals_wrap()
    ex.orbitals_on()
    ex.third(1, (1, 3, 2))
    ex.second(0)
    ex.orbitals_done()
    prepare()
    slots.wait()
    ex.ready(1)
    mixed(1)
    ex.third(2, (1, 3, 2))
    low(1)
    high(1)
    ex.third(0, (1, 3, 2))
    ex.ready(2)
    mixed(2)
    low(2)
    high(2)
    ex.ready(0)
    mixed(0)
    low(0)
    ex.finish()


def body(orbitals, screen, slot_of_q):
    vmem = pl.BlockSpec(memory_space=pltpu.VMEM)
    leaves, tree = jax.tree.flatten((scratch(), buffers(), exchange_sems()))
    lower, upper = pl.pallas_call(
        functools.partial(kernel, tree),
        out_shape=[
            jax.ShapeDtypeStruct((1, 3, 2, 96, 384), BF),
            jax.ShapeDtypeStruct((1, 2, 2, 96, 384), BF),
        ],
        in_specs=[pl.BlockSpec(memory_space=pltpu.HBM)] * 3,
        out_specs=[vmem] * 2,
        scratch_shapes=leaves,
        compiler_params=pltpu.CompilerParams(collective_id=0, has_side_effects=True, vmem_limit_bytes=56 << 20),
        name="pairs",
    )(slot_of_q, screen.reshape(2, 24, 32, 128), orbitals)
    return jnp.swapaxes(lower, 3, 4), upper


def solution(mesh):
    in_specs = (P(("blk", "grp"), None, None, None), P("blk", "grp", None, None, None), P())
    out_specs = (P("blk", None, None, None, "grp"), P("blk", None, None, "grp", None))
    return jax.shard_map(body, mesh=mesh, in_specs=in_specs, out_specs=out_specs, check_vma=False)
```

```python
import functools
import jax
import jax.numpy as jnp
from jax import lax
from jax.experimental import pallas as pl
from jax.experimental.pallas import tpu as pltpu
from jax.sharding import PartitionSpec as P

BF = jnp.bfloat16
F32 = jnp.float32


def select_matrix(tile):
    r = lax.broadcasted_iota(jnp.int32, (256, 128), 0)
    col = lax.broadcasted_iota(jnp.int32, (256, 128), 1)
    band = (r % 4) if tile else ((r // 4) % 4)
    return (col == (r // 16) * 8 + 4 + band).astype(F32).astype(BF)


def expand_rows(x, dst, stage, sel):
    x2 = x.reshape(384, 128)
    for i in range(3):
        dst[pl.ds(i * 256, 256), :] = jnp.dot(sel, x2[i * 128:(i + 1) * 128], preferred_element_type=F32)
    stage[...] = x2.astype(F32)


def valence(stage, dst):
    for p in range(2):
        for v in range(4):
            dst[p * 4 + v] = stage[pl.ds(p * 8 + v, 24, stride=16), :]


def expand_cols(x, dst, pt, sel):
    x2 = x.reshape(96, 128)
    dst[...] = jnp.dot(sel[:192, :96], x2, preferred_element_type=F32)
    n = lax.broadcasted_iota(jnp.int32, (8, 128), 0)
    l = lax.broadcasted_iota(jnp.int32, (8, 128), 1)
    g = (n == l % 4).astype(F32)
    dn = (((0,), (0,)), ((), ()))
    for j in range(6):
        a = lax.dot_general(x[j, 0].astype(F32), g, dn, preferred_element_type=F32).astype(BF)
        b = lax.dot_general(x[j, 1].astype(F32), g, dn, preferred_element_type=F32).astype(BF)
        pt[j, 0:128, 0:128] = a
        pt[j, 0:128, 128:256] = -b
        pt[j, 128:256, 0:128] = b
        pt[j, 128:256, 128:256] = a


def mix(load_w, slot_ref, s, g6, jobs):
    def step(q, carry):
        wr, wi = load_w(slot_ref[s, q])
        wc = jnp.concatenate([jnp.concatenate([wr, wi], 1), jnp.concatenate([-wi, wr], 1)], 0)
        rows = []
        for urep, utile, _, _ in jobs:
            for j in range(6):
                k = lax.rem(g6 + j + q, 24)
                at = pl.multiple_of(k * 32, 32)
                ar = urep[pl.ds(at, 16), :]
                ai = urep[pl.ds(at + 16, 16), :]
                br = utile[j * 32:j * 32 + 16, :]
                bi = utile[j * 32 + 16:j * 32 + 32, :]
                rows.append(jnp.concatenate([(ar * br + ai * bi).astype(BF), (ar * bi - ai * br).astype(BF)], 1))
        y = jnp.dot(jnp.concatenate(rows, 0), wc, preferred_element_type=F32)
        for n, (_, _, yr, yi) in enumerate(jobs):
            for j in range(6):
                k = lax.rem(g6 + j + q, 24)
                r0 = (n * 6 + j) * 16
                yr[pl.ds(j * 384 + k, 16, stride=24), :] = y[r0:r0 + 16, 0:128]
                yi[pl.ds(j * 384 + k, 16, stride=24), :] = y[r0:r0 + 16, 128:256]
        return carry
    lax.fori_loop(0, 24, step, 0, unroll=8)


def close(yr, yi, uv, pt, acc, tr, ti):
    lane = lax.broadcasted_iota(jnp.int32, (256, 256), 1) % 128 // 4

    def step(j, carry):
        ur = uv[0:4]
        ui = uv[4:8]
        p = pt[j]
        weights = jnp.concatenate([jnp.where(lane == j * 4 + c2, p, jnp.zeros_like(p)) for c2 in range(4)], 0)
        blocks = []
        for c in range(4):
            parts = []
            for c2 in range(4):
                at = pl.multiple_of(j * 384 + (c * 4 + c2) * 24, 8)
                a = yr[pl.ds(at, 24), :][None]
                b = yi[pl.ds(at, 24), :][None]
                parts.append((a * ur - b * ui).reshape(96, 128).astype(BF))
                parts.append((a * ui + b * ur).reshape(96, 128).astype(BF))
            blocks.append(jnp.concatenate(parts, 1))
        d = jnp.dot(jnp.concatenate(blocks, 0), weights, preferred_element_type=F32)

        acc[...] += d
        return carry
    acc[...] = jnp.zeros_like(acc)
    lax.fori_loop(0, 6, step, 0, unroll=6)
    for cv in range(16):
        tr[pl.ds(cv, 24, stride=16), :] = acc[cv * 24:cv * 24 + 24, 0:128]
        ti[pl.ds(cv, 24, stride=16), :] = acc[cv * 24:cv * 24 + 24, 128:256]


def emit_lower(tr, ti, out, s):
    out[0, s, 0] = tr[...].T[0:96, :].astype(BF)
    out[0, s, 1] = ti[...].T[0:96, :].astype(BF)


def emit_upper(tr, ti, out, t):
    out[0, t, 0] = tr[...].T[0:96, :].astype(BF)
    out[0, t, 1] = (-ti[...]).T[0:96, :].astype(BF)


def scratch():
    return dict(
        urep=[pltpu.VMEM((768, 128), F32)] * 3,
        uv=[pltpu.VMEM((8, 24, 128), F32)] * 3,
        utile=[pltpu.VMEM((192, 128), F32)] * 3,
        pt=[pltpu.VMEM((6, 256, 256), BF)] * 3,
        stage=pltpu.VMEM((384, 128), F32),
        yr=[pltpu.VMEM((2304, 128), F32)] * 2,
        yi=[pltpu.VMEM((2304, 128), F32)] * 2,
        acc=pltpu.VMEM((384, 256), F32),
        tr=pltpu.VMEM((384, 128), F32),
        ti=pltpu.VMEM((384, 128), F32),
    )


MESH = pl.DeviceIdType.MESH


def place():
    b = lax.axis_index("blk")
    g = lax.axis_index("grp")
    return (b // 16) % 4, (b // 64) * 2 + g // 2, b % 16, g % 2


def at_chip(x, y, z, c):
    x, y, z = lax.rem(x, 4), lax.rem(y, 4), lax.rem(z, 16)
    return (y // 2) * 64 + x * 16 + z, (y % 2) * 2 + c


class Exchange:
    def __init__(self, screen, orb, wbuf, rows, subs, sems):
        self.screen, self.orb, self.wbuf, self.rows, self.subs = screen, orb, wbuf, rows, subs
        self.sems = sems
        self.x, self.y, self.z, self.c = place()
        self.b, self.g = lax.axis_index("blk"), lax.axis_index("grp")
        self.h = jnp.where((self.y == 1) | (self.y == 2), 1, 0)
        self.yh = self.y // 2
        self.source = (self.x == 0) & (self.y < 2) & (self.z < 3)
        self.pending = []

    def row(self, off):
        return lax.rem(self.b + off + 128, 128)

    def signal(self, sem, to, cond=None):
        def go():
            pl.semaphore_signal(sem, inc=1, device_id=to, device_id_type=MESH)
        if cond is None:
            go()
        else:
            pl.when(cond)(go)

    def barrier(self):
        bar = pltpu.get_barrier_semaphore()
        x, y, z, c, g = self.x, self.y, self.z, self.c, self.g
        near = [at_chip(x + d, y, z, c) for d in (1, 2, 3)] + [at_chip(x, y + d, z, c) for d in (1, 2, 3)]
        near += [(self.b, lax.rem(g + d, 4)) for d in (1, 3)]
        for d in near:
            self.signal(bar, d)

        @pl.when(self.source)
        def _():
            for xx in range(4):
                for yh in range(2):
                    if xx or yh:
                        self.signal(bar, self.target(xx, yh))
        self.signal(bar, at_chip(0, self.h, z, c), (z < 3) & jnp.logical_not(self.source))
        for k in (1, 2, 3):
            self.signal(bar, at_chip(x, y, z + k, c), z + k < 16)
        self.signal(bar, at_chip(x, y, 15, c), z == 0)
        self.signal(bar, (self.row(-1), g), z == 0)
        self.signal(bar, (self.row(-2), g), z < 2)
        count = len(near) + jnp.where(self.source, 7, jnp.where(z < 3, 1, 0))
        count += jnp.minimum(z, 3) + jnp.where(z == 15, 3, jnp.where(z == 14, 1, 0))
        pl.semaphore_wait(bar, count)
        for k in (1, 2, 3):
            self.signal(self.sems["rdyz"].at[k - 1], at_chip(x, y, z + 16 - k, c), z >= k)
        self.signal(self.sems["rdyw"], at_chip(x, y, 0, c), z == 15)
        self.signal(self.sems["rdyr"].at[0], (self.row(1), g), z == 15)
        self.signal(self.sems["rdyr"].at[1], (self.row(2), g), z >= 14)

    def await_up(self, s, only=None):
        z = self.z
        for k in (1, 2, 3):
            early = {1: ((z == 1) & (k < 3)) | ((z == 3) & (k != 2)) | (z == 6) | ((z == 9) & (k == 1)),
                     2: (z == 2) & (k == 1), 0: z == 0}
            if s is None:
                cond = (z + k < 16) & jnp.logical_not(early[0] | early[1] | early[2])
            else:
                cond = early[s] if only is None else early[s] & only
            pl.when(cond)(lambda k=k: pl.semaphore_wait(self.sems["rdyz"].at[k - 1], 1))

    def target(self, xx, yh):
        return at_chip(xx, self.y if yh == 0 else 3 - self.y, self.z, self.c)

    def remote(self, src, dst, send, recv, to):
        return pltpu.make_async_remote_copy(src_ref=src, dst_ref=dst, send_sem=send, recv_sem=recv, device_id=to, device_id_type=MESH)

    def launch(self, cp, cond=None):
        if cond is None:
            cp.start()
        else:
            pl.when(cond)(lambda: cp.start())
        self.pending.append((cp, cond))

    def unit(self, half, x):
        return pl.ds(half * 12 + x * 3, 3)

    def own(self, s, half):
        return self.wbuf[s].at[self.h, self.c, self.yh, self.unit(half, self.x)]

    def scattered(self, s):
        sm = self.sems
        for half in range(2):
            for xx, yh in ((2, 1), (1, 1), (3, 1), (2, 0), (1, 0), (3, 0), (0, 1)):
                yield self.remote(self.screen.at[yh, self.unit(half, xx)], self.wbuf[s].at[self.h, self.c, yh, self.unit(half, xx)],
                                  sm["scat"].at[half, xx, yh], sm["own"].at[s, half], self.target(xx, yh))

    def scatter(self):
        for s in range(3):
            @pl.when(self.source & (self.z == s))
            def _():
                for cp in self.scattered(s):
                    cp.start()
                for half in range(2):
                    pltpu.make_async_copy(self.screen.at[0, self.unit(half, 0)], self.wbuf[s].at[self.h, self.c, 0, self.unit(half, 0)],
                                          self.sems["own"].at[s, half]).start()

    def drain_scatter(self):
        for s in range(3):
            @pl.when(self.source & (self.z == s))
            def _():
                for cp in self.scattered(s):
                    cp.wait_send()

    def orbitals_out(self):
        sm, g = self.sems, self.g
        self.o_in = []
        self.o_local = [pltpu.make_async_copy(self.orb, self.rows.at[0, pl.ds(g * 6, 6)], sm["oloc"].at[0]),
                        pltpu.make_async_copy(self.orb, self.subs.at[0], sm["oloc"].at[1])]
        for cp in self.o_local:
            cp.start()
        self.o_row = []
        for n, (off, dst) in enumerate(((-1, self.rows.at[1, pl.ds(g * 6, 6)]), (-2, self.rows.at[2, pl.ds(g * 6, 6)]),
                                        (1, self.subs.at[1]), (2, self.subs.at[2]))):
            self.o_row.append(self.remote(self.orb, dst, sm["os"].at[n], sm["or"].at[n], (self.row(off), g)))
        self.group_out(0, self.orb, 4)
        z = self.z
        self.launch(self.o_row[0], z >= 1)
        self.launch(self.o_row[1], z >= 2)
        self.launch(self.o_row[2], z == 15)
        self.launch(self.o_row[3], z >= 14)

    def orbitals_up(self):
        self.launch(self.o_row[2], self.z < 15)
        self.launch(self.o_row[3], self.z < 14)

    def orbitals_wrap(self):
        z = self.z
        pl.when(z == 0)(lambda: pl.semaphore_wait(self.sems["rdyr"].at[0], 1))
        pl.when(z < 2)(lambda: pl.semaphore_wait(self.sems["rdyr"].at[1], 1))
        self.launch(self.o_row[0], z == 0)
        self.launch(self.o_row[1], z < 2)

    def group_out(self, r, src, base):
        for d in (1, 2, 3):
            n = base + d - 1
            cp = self.remote(src, self.rows.at[r, pl.ds(self.g * 6, 6)], self.sems["os"].at[n], self.sems["or"].at[n],
                             (self.b, lax.rem(self.g + d, 4)))
            self.launch(cp)
            back = lax.rem(self.g + 4 - d, 4)
            self.o_in.append(self.remote(src, self.rows.at[r, pl.ds(back * 6, 6)], self.sems["os"].at[n], self.sems["or"].at[n],
                                         (self.b, lax.rem(self.g + d, 4))))

    def orbitals_on(self):
        for r in (1, 2):
            self.o_row[r - 1].wait_recv()
            self.group_out(r, self.rows.at[r, pl.ds(self.g * 6, 6)], 4 + 3 * r)

    def orbitals_near(self):
        for cp in self.o_local:
            cp.wait()
        for cp in self.o_row[2:] + self.o_in[:3]:
            cp.wait_recv()

    def orbitals_done(self):
        for cp in self.o_in[3:]:
            cp.wait_recv()

    def first(self, s, only=None):
        sm, x, y, z, c = self.sems, self.x, self.y, self.z, self.c
        hops = ((3, (z == 3) | (z == 6) | (z == (0 if s == 0 else 3))), (2, (z == 6) | (z == (s if s < 2 else 6))),
                (15, (z == 6) | (z == 15) | (z == 12) | (z == (s if s else 6))), (13, z == 15),
                (14, (z == 15) | (z == (2 if s == 2 else 15))), (1, (z == 3) | (z == 6) | (z == 9) | (z == s)))
        for half in range(2):
            mine = self.own(s, half)
            cp = self.remote(mine, mine, sm["zs"].at[s, 0, half], sm["own"].at[s, half], (self.b, self.g))
            if only is None:
                cp.wait_recv()
            else:
                pl.when(only)(cp.wait_recv)
            if half == 0:
                self.await_up(s, only)
            for n, (off, cond) in enumerate(hops):
                cond = cond if only is None else cond & only
                self.launch(self.remote(mine, mine, sm["zs"].at[s, n, half], sm["own"].at[s, half], at_chip(x, y, z + off, c)), cond)
            for d in (2, 1, 3):
                to = at_chip(x + d, y, z, c) if half == 0 else at_chip(x, y + d, z, c)
                self.launch(self.remote(mine, mine, sm["p1s"].at[s, half, d - 1], sm["p1r"].at[s, half, d - 1], to), only)

    def down(self, s):
        sm, z = self.sems, self.z
        if s == 1:
            pl.when(z == 0)(lambda: pl.semaphore_wait(sm["rdyw"], 1))
        for half in range(2):
            mine = self.own(s, half)
            self.launch(self.remote(mine, mine, sm["ds"].at[s, half], sm["own"].at[s, half], at_chip(self.x, self.y, 15, self.c)), z == 0)

    def split(self, y):
        return jnp.where((y == 1) | (y == 2), 1, 0), y // 2

    def part(self, s, half, d, c):
        if half == 0:
            hh, yy = self.split(lax.rem(self.y + 4 - d, 4))
            return self.wbuf[s].at[hh, c, yy, pl.ds(0, 12)]
        return self.wbuf[s].at[:, c, :, self.unit(1, lax.rem(self.x + 4 - d, 4))]

    def to_sibling(self, s, half, d):
        mine = self.part(s, half, d, self.c)
        self.launch(self.remote(mine, mine, self.sems["cs"].at[s, half, d], self.sems["cr"].at[s, half, d],
                                at_chip(self.x, self.y, self.z, 1 - self.c)))

    def second(self, s):
        sm, x, y, z, c = self.sems, self.x, self.y, self.z, self.c
        for half in range(2):
            for d in (1, 3, 2):
                if half == 0:
                    there = self.wbuf[s].at[self.h, c, self.yh, self.unit(0, lax.rem(x + 4 - d, 4))]
                else:
                    hh, yy = self.split(lax.rem(y + 4 - d, 4))
                    there = self.wbuf[s].at[hh, c, yy, self.unit(1, x)]
                self.remote(there, there, sm["p1s"].at[s, half, d - 1], sm["p1r"].at[s, half, d - 1], (self.b, self.g)).wait_recv()
            mine = self.part(s, half, 0, c)
            for d in (2, 1, 3):
                to = at_chip(x, y + d, z, c) if half == 0 else at_chip(x + d, y, z, c)
                self.launch(self.remote(mine, mine, sm["p2s"].at[s, half, d - 1], sm["p2r"].at[s, half, d - 1], to))
            self.to_sibling(s, half, 0)

    def third(self, s, steps):
        sm = self.sems
        for d in steps:
            for half in range(2):
                there = self.part(s, half, d, self.c)
                self.remote(there, there, sm["p2s"].at[s, half, d - 1], sm["p2r"].at[s, half, d - 1], (self.b, self.g)).wait_recv()
                self.to_sibling(s, half, d)

    def ready(self, s):
        for d in (0, 1, 3, 2):
            for half in range(2):
                there = self.part(s, half, d, 1 - self.c)
                self.remote(there, there, self.sems["cs"].at[s, half, d], self.sems["cr"].at[s, half, d], (self.b, self.g)).wait_recv()

    def finish(self):
        self.drain_scatter()
        for cp, cond in self.pending:
            if cond is None:
                cp.wait_send()
            else:
                pl.when(cond)(lambda cp=cp: cp.wait_send())


def exchange_sems():
    D = pltpu.SemaphoreType.DMA
    return {"scat": D((2, 4, 2)), "own": D((3, 2)), "zs": D((3, 6, 2)), "p1s": D((3, 2, 3)), "p1r": D((3, 2, 3)),
            "p2s": D((3, 2, 3)), "p2r": D((3, 2, 3)), "cs": D((3, 2, 4)), "cr": D((3, 2, 4)), "ds": D((3, 2)), "os": D((13,)), "or": D((13,)), "oloc": D((2,)),
            "rdyz": pltpu.SemaphoreType.REGULAR((3,)), "rdyw": pltpu.SemaphoreType.REGULAR, "rdyr": pltpu.SemaphoreType.REGULAR((2,))}


def buffers():
    return {"w": [pltpu.VMEM((2, 2, 2, 24, 32, 128), BF)] * 3, "rows": pltpu.VMEM((3, 24, 2, 8, 128), BF), "subs": pltpu.VMEM((3, 6, 2, 8, 128), BF),
            "slot": pltpu.SMEM((3, 24), jnp.int32), "slot_sem": pltpu.SemaphoreType.DMA}


def kernel(tree, slot_ref, screen, orb, lower, upper, *flat):
    sc, buf, sems = jax.tree.unflatten(tree, flat)
    w_ref, slot_sm = buf["w"], buf["slot"]
    g6 = lax.axis_index("grp") * 6
    ex = Exchange(screen, orb, w_ref, buf["rows"], buf["subs"], sems)

    def prepare_rows(r):
        expand_rows(buf["rows"][r], sc["urep"][r], sc["stage"], select_matrix(False))
        valence(sc["stage"], sc["uv"][r])

    def prepare():
        prepare_rows(0)
        tile = select_matrix(True)
        for r in range(3):
            expand_cols(buf["subs"][r], sc["utile"][r], sc["pt"][r], tile)

    def near():
        ex.orbitals_near()
        prepare()

    def jobs_of(s):
        jobs = [(sc["urep"][0], sc["utile"][s], sc["yr"][0], sc["yi"][0])]
        if s:
            jobs.append((sc["urep"][s], sc["utile"][0], sc["yr"][1], sc["yi"][1]))
        return jobs

    def mixed(s):
        def load_w(slot):
            part = slot // 3
            w = w_ref[s][part // 4, part // 2 % 2, part % 2, pl.ds(slot % 3 * 8, 8)]
            return w[0:4].reshape(128, 128), w[4:8].reshape(128, 128)
        mix(load_w, slot_sm, s, g6, jobs_of(s))

    def low(s):
        close(sc["yr"][0], sc["yi"][0], sc["uv"][0], sc["pt"][s], sc["acc"], sc["tr"], sc["ti"])
        emit_lower(sc["tr"], sc["ti"], lower, s)

    def high(s):
        close(sc["yr"][1], sc["yi"][1], sc["uv"][s], sc["pt"][0], sc["acc"], sc["tr"], sc["ti"])
        emit_upper(sc["tr"], sc["ti"], upper, s - 1)

    slots = pltpu.make_async_copy(slot_ref, slot_sm, buf["slot_sem"])
    slots.start()
    ex.barrier()
    ex.scatter()
    ex.orbitals_out()
    ex.first(1)
    ex.down(1)
    ex.await_up(None)
    ex.orbitals_up()
    ex.first(2)
    ex.down(2)
    ex.first(0, ex.z == 0)
    ex.down(0)
    ex.second(1)
    pl.when(ex.z <= 9)(near)
    ex.first(0, ex.z > 0)
    ex.second(2)
    ex.orbitals_wrap()
    ex.orbitals_on()
    ex.third(1, (1, 3, 2))
    ex.second(0)
    pl.when(ex.z > 9)(near)
    ex.orbitals_done()
    prepare_rows(1)
    prepare_rows(2)
    slots.wait()
    ex.ready(1)
    mixed(1)
    ex.third(2, (1, 3, 2))
    low(1)
    high(1)
    ex.third(0, (1, 3, 2))
    ex.ready(2)
    mixed(2)
    low(2)
    high(2)
    ex.ready(0)
    mixed(0)
    low(0)
    ex.finish()


def body(orbitals, screen, slot_of_q):
    vmem = pl.BlockSpec(memory_space=pltpu.VMEM)
    leaves, tree = jax.tree.flatten((scratch(), buffers(), exchange_sems()))
    lower, upper = pl.pallas_call(
        functools.partial(kernel, tree),
        out_shape=[
            jax.ShapeDtypeStruct((1, 3, 2, 96, 384), BF),
            jax.ShapeDtypeStruct((1, 2, 2, 96, 384), BF),
        ],
        in_specs=[pl.BlockSpec(memory_space=pltpu.HBM)] * 3,
        out_specs=[vmem] * 2,
        scratch_shapes=leaves,
        compiler_params=pltpu.CompilerParams(collective_id=0, has_side_effects=True, vmem_limit_bytes=56 << 20),
        name="pairs",
    )(slot_of_q, screen.reshape(2, 24, 32, 128), orbitals)
    return jnp.swapaxes(lower, 3, 4), upper


def solution(mesh):
    in_specs = (P(("blk", "grp"), None, None, None), P("blk", "grp", None, None, None), P())
    out_specs = (P("blk", None, None, None, "grp"), P("blk", None, None, "grp", None))
    return jax.shard_map(body, mesh=mesh, in_specs=in_specs, out_specs=out_specs, check_vma=False)
```
